256 devices in a mesh: tenant: 16 (over x, z_hi, core), tensor: 16 (over z_lo, y).
Axes of the slice: x: 4, y: 4, z: 8 (z_hi: 2, z_lo: 4; z = z_hi * 4 + z_lo), core: 2. Of those that a mesh axis runs over, the one named last changes fastest.
Arguments:
- projection_input: bfloat16 [8192, 8192], P('tenant', 'tensor'), may hold values from -6 to 6
- output_gradient: bfloat16 [8192, 8192], P('tenant', 'tensor'), may hold values from -6 to 6
- frozen_weight: bfloat16 [8192, 8192], P('tenant', 'tensor'), may hold values from -0.0625 to 0.0625
- down_adapters: bfloat16 [16, 64, 8192], P('tenant', None, 'tensor'), may hold values from -0.0625 to 0.0625
- up_adapters: bfloat16 [16, 64, 8192], P('tenant', None, 'tensor'), may hold values from -0.0625 to 0.0625
- lengths: int32 [16], P('tenant'), may hold values from 128 to 512, as said below
Outputs:
- grad_input: bfloat16 [8192, 8192], P('tenant', 'tensor')
- down_gradient: float32 [16, 64, 8192], P('tenant', None, 'tensor')
- up_gradient: float32 [16, 64, 8192], P('tenant', None, 'tensor')
The draws below stay inside these ranges and needn't reach their ends.
Inputs may be any that keep to these rules, and one draw needn't show every extreme that they name: `lengths`: each entry is a multiple of 128; some tenant has exactly 512 live tokens.
All inputs are finite; a program needn't handle non-finite values.
Results may differ from the reference program's by a relative error of at most 0.001.
Values may be sent and summed in bfloat16 or wider, within the bound.
No kernel may reach another device: no remote copies, remote signals or barrier semaphores. Data moves between devices by JAX's collectives and lax.ppermute only.
A program may use at most 128 MiB of HBM per device.

```python
import jax
import jax.numpy as jnp
from jax import lax

MODEL_WIDTH = 8192
ADAPTER_RANK = 64
BLOCK = 128
TOK_DEV = 512
TENANT_TOTAL = 16
TOKENS = 8192


def draw_lengths(key, part):
    key = jax.random.fold_in(key, 7)
    first_key, second_key = jax.random.split(key)
    blocks = TOK_DEV // BLOCK
    counts = jax.random.randint(first_key, (TENANT_TOTAL,), 1, blocks + 1)
    full_index = jax.random.randint(second_key, (), 0, TENANT_TOTAL)
    counts = jnp.where(jnp.arange(TENANT_TOTAL) == full_index, blocks, counts)
    return (counts * BLOCK).astype(jnp.int32)


def levels(own_key, dims, cuts, least, top_value):
    level = 1.0
    for dim, blocks in cuts:
        draws = jax.random.uniform(jax.random.fold_in(jax.random.fold_in(own_key, 6), dim), (blocks,), jnp.float32, least / len(cuts), top_value / len(cuts))
        level = level * jnp.repeat(jnp.exp(draws), dims[dim] // blocks).reshape((-1,) + (1,) * (len(dims) - 1 - dim))
    return level


def bell_draw(own_key, dims, spread, limit, cuts=(), kind=jnp.bfloat16):
    array = spread * jax.random.normal(own_key, dims, jnp.float32)
    if cuts:
        array = array * levels(own_key, dims, cuts, -0.22, 0.18)
    return jnp.clip(array, -limit, limit).astype(kind)


def setup_inputs(seed: int = 0) -> dict:
    streams_of = jax.random.split(jax.random.key(seed), 7)
    return {
        "projection_input": bell_draw(streams_of[0], (TOKENS, MODEL_WIDTH), 1.0, 6.0, ((0, 16), (1, 16))),
        "output_gradient": bell_draw(streams_of[1], (TOKENS, MODEL_WIDTH), 1.0, 6.0, ((0, 16), (1, 16))),
        "frozen_weight": bell_draw(streams_of[2], (MODEL_WIDTH, MODEL_WIDTH), MODEL_WIDTH ** -0.5, 0.0625, ((0, 16), (1, 16))),
        "down_adapters": bell_draw(streams_of[3], (TENANT_TOTAL, ADAPTER_RANK, MODEL_WIDTH), MODEL_WIDTH ** -0.5, 0.0625, ((0, 16), (2, 16))),
        "up_adapters": bell_draw(streams_of[4], (TENANT_TOTAL, ADAPTER_RANK, MODEL_WIDTH), MODEL_WIDTH ** -0.5, 0.0625, ((0, 16), (2, 16))),
        "lengths": draw_lengths(jax.random.fold_in(streams_of[6], 71), 0),
    }


adapter_scale = 2.0


def reference(projection_input, output_gradient, frozen_weight, down_adapters, up_adapters, lengths):
    positions = jnp.arange(TOK_DEV, dtype=jnp.int32)
    input_stack = projection_input.reshape(TENANT_TOTAL, TOK_DEV, MODEL_WIDTH)
    gradient_stack = output_gradient.reshape(TENANT_TOTAL, TOK_DEV, MODEL_WIDTH)
    highest = lax.Precision.HIGHEST

    def tenant_backward(tenant_args):
        inputs, out_rows, down_adapter, up_adapter, token_count = tenant_args
        kept_rows = (positions < token_count).astype(out_rows.dtype)[:, None]
        masked_rows = out_rows * kept_rows
        rank_projected = jnp.dot(inputs, down_adapter.T, preferred_element_type=jnp.float32)
        pulled_rows = jnp.dot(masked_rows, up_adapter.T, preferred_element_type=jnp.float32)
        scaled_gradient = adapter_scale * pulled_rows
        base_part = lax.dot_general(masked_rows, frozen_weight, (((1,), (1,)), ((), ())), preferred_element_type=jnp.float32)
        adapter_part = jnp.dot(scaled_gradient, down_adapter.astype(jnp.float32), precision=highest)
        input_gradient = (base_part + adapter_part).astype(jnp.bfloat16)
        inverse_order = 1.0 / token_count.astype(jnp.float32)
        grad_down = jnp.dot(scaled_gradient.T, inputs.astype(jnp.float32), precision=highest) * inverse_order
        up_rank_gradient = adapter_scale * jnp.dot(rank_projected.T, masked_rows.astype(jnp.float32), precision=highest) * inverse_order
        return input_gradient, grad_down, up_rank_gradient

    input_gradient, down_gradient, up_gradient = lax.map(tenant_backward, (input_stack, gradient_stack, down_adapters, up_adapters, lengths))
    return input_gradient.reshape(TOKENS, MODEL_WIDTH), down_gradient, up_gradient
```

```python
import itertools

import jax
import jax.numpy as jnp
from jax import lax
from jax.experimental import pallas as pl
from jax.experimental.pallas import tpu as pltpu
from jax.sharding import Mesh, PartitionSpec as P

adapter_scale = 2.0
AXES = ("x", "zh", "c", "zl", "y")
SIZES = (4, 2, 2, 4, 4)
DIM = 512
HALF = 256


def moves(target):
    pairs = []
    for source, place in enumerate(itertools.product(*[range(n) for n in SIZES])):
        index = 0
        for n, i in zip(SIZES, target(*place)):
            index = index * n + i % n
        pairs.append((source, index))
    return pairs


def send(value, target):
    return lax.ppermute(value, AXES, moves(target))


def way(c):
    return 1 - 2 * c


def product_kernel(slot_ref, *refs):
    g_refs, w_refs = refs[:16], refs[16:32]
    add_ref, kept_ref, out_ref, gs, ws, acc, g_sems, w_sems = refs[32:]
    for i in range(16):
        pltpu.make_async_copy(g_refs[i], gs.at[i], g_sems.at[i]).start()
    for i in range(16):
        for h in range(2):
            slot = slot_ref[16 + 2 * i + h]
            rows = pl.ds(h * HALF, HALF)
            pltpu.make_async_copy(w_refs[i].at[rows], ws.at[slot, rows], w_sems.at[h, slot]).start()
    acc[...] = jnp.zeros_like(acc)

    def step(i, carry):
        slot = slot_ref[i]
        pltpu.make_async_copy(gs.at[i], gs.at[i], g_sems.at[i]).wait()
        for h in range(2):
            rows = pl.ds(h * HALF, HALF)
            pltpu.make_async_copy(ws.at[slot, rows], ws.at[slot, rows], w_sems.at[h, slot]).wait()
        acc[...] += lax.dot_general(
            gs[i], ws[slot], (((1,), (1,)), ((), ())), preferred_element_type=jnp.float32
        )
        return carry

    lax.fori_loop(0, 16, step, 0)
    out_ref[...] = (acc[...] * kept_ref[...] + add_ref[...]).astype(out_ref.dtype)


def shards(projection_input, output_gradient, frozen_weight, down_adapters, up_adapters, lengths):
    tokens = output_gradient.shape[0]
    highest = lax.Precision.HIGHEST
    x, zh, c, zl, y = (lax.axis_index(a) for a in AXES)
    turn = way(c)

    parts = {}
    for s in range(2):
        for r in (0, 2):
            h = r // 2
            parts[s, r] = send(
                frozen_weight[h * HALF : (h + 1) * HALF],
                lambda x, zh, c, zl, y: (zl + r, (y // 2) ^ s, y % 2, x, 2 * zh + c),
            )
    own = [[jnp.concatenate([parts[s, 0], parts[s, 2]], axis=0)] for s in range(2)]
    for t in range(3):
        for s in range(2):
            own[s].append(send(own[s][-1], lambda x, zh, c, zl, y: (x + way(c), zh, c, zl, y)))
    other = [[send(v, lambda x, zh, c, zl, y: (x, zh, 1 - c, zl, y)) for v in own[s]] for s in range(2)]

    blocks = []
    for j in range(4):
        here = output_gradient if j == 0 else send(
            output_gradient, lambda x, zh, c, zl, y: (x, zh, c, zl + j, y)
        )
        behind = send(here, lambda x, zh, c, zl, y: (x, zh, c, zl, y + way(c)))
        ahead = send(here, lambda x, zh, c, zl, y: (x, zh, c, zl, y - way(c)))
        across = send(behind, lambda x, zh, c, zl, y: (x, zh, c, zl, y + way(c)))
        source_zl = (zl - j) % 4
        blocks += [
            (here, source_zl, y),
            (behind, source_zl, (y - turn) % 4),
            (ahead, source_zl, (y + turn) % 4),
            (across, source_zl, (y + 2) % 4),
        ]

    slots = [4 * block_zl + block_y for _, block_zl, block_y in blocks]
    weights = []
    for held, core, direction in ((own, c, turn), (other, 1 - c, -turn)):
        for s in range(2):
            for t in range(4):
                from_x = x - t * direction
                block_y = 2 * (zh ^ s) + core
                weights.append(held[s][t])
                slots += [4 * (from_x % 4) + block_y, 4 * ((from_x - 2) % 4) + block_y]
    slots = jnp.stack([jnp.asarray(v, jnp.int32) for v in slots])

    positions = lax.iota(jnp.int32, tokens)
    kept = positions < lengths[0]
    masked_rows = output_gradient * kept.astype(output_gradient.dtype)[:, None]
    down_adapter = down_adapters[0]
    up_adapter = up_adapters[0]
    rank_width = down_adapter.shape[0]
    lowered_part = jnp.dot(projection_input, down_adapter.T, preferred_element_type=jnp.float32)
    pulled_part = jnp.dot(masked_rows, up_adapter.T, preferred_element_type=jnp.float32)
    rank_both = jnp.concatenate([lowered_part, pulled_part], axis=1)
    for target in (
        lambda x, zh, c, zl, y: (x, zh, c, zl, y ^ 1),
        lambda x, zh, c, zl, y: (x, zh, c, zl, y ^ 3),
        lambda x, zh, c, zl, y: (x, zh, c, zl ^ 1, y),
        lambda x, zh, c, zl, y: (x, zh, c, zl ^ 2, y),
    ):
        rank_both = rank_both + send(rank_both, target)
    rank_projected = rank_both[:, :rank_width]
    scaled_gradient = adapter_scale * rank_both[:, rank_width:]
    adapter_part = jnp.dot(scaled_gradient, down_adapter.astype(jnp.float32), precision=highest)
    inverse_order = 1.0 / lengths[0].astype(jnp.float32)
    down_gradient = (
        jnp.dot(scaled_gradient.T, projection_input.astype(jnp.float32), precision=highest)
        * inverse_order
    )[None]
    up_gradient = (
        adapter_scale
        * jnp.dot(rank_projected.T, masked_rows.astype(jnp.float32), precision=highest)
        * inverse_order
    )[None]

    anywhere = pl.BlockSpec(memory_space=pl.ANY)
    in_vmem = pl.BlockSpec(memory_space=pltpu.VMEM)
    grad_input = pl.pallas_call(
        product_kernel,
        out_shape=jax.ShapeDtypeStruct((tokens, DIM), jnp.bfloat16),
        in_specs=[pl.BlockSpec(memory_space=pltpu.SMEM)] + [anywhere] * 32 + [in_vmem] * 2,
        out_specs=in_vmem,
        scratch_shapes=[
            pltpu.VMEM((16, tokens, DIM), jnp.bfloat16),
            pltpu.VMEM((16, DIM, DIM), jnp.bfloat16),
            pltpu.VMEM((tokens, DIM), jnp.float32),
            pltpu.SemaphoreType.DMA((16,)),
            pltpu.SemaphoreType.DMA((2, 16)),
        ],
        compiler_params=pltpu.CompilerParams(vmem_limit_bytes=32 * 1024 * 1024),
        cost_estimate=pl.CostEstimate(
            flops=2 * tokens * DIM * DIM * 16, bytes_accessed=18 * 1024 * 1024, transcendentals=0
        ),
    )(slots, *[b[0] for b in blocks], *weights, adapter_part, kept.astype(jnp.float32)[:, None])
    return (grad_input, down_gradient, up_gradient)


def solution(mesh):
    parts = Mesh(mesh.devices.reshape(SIZES), AXES)
    tenant, tensor = ("x", "zh", "c"), ("zl", "y")
    placed = (
        P(tenant, tensor),
        P(tenant, tensor),
        P(tenant, tensor),
        P(tenant, None, tensor),
        P(tenant, None, tensor),
        P(tenant),
    )
    return jax.shard_map(
        shards,
        mesh=parts,
        in_specs=placed,
        out_specs=(P(tenant, tensor), P(tenant, None, tensor), P(tenant, None, tensor)),
        check_vma=False,
    )
```

```python
import itertools

import jax
import jax.numpy as jnp
from jax import lax
from jax.experimental import pallas as pl
from jax.experimental.pallas import tpu as pltpu
from jax.sharding import Mesh, PartitionSpec as P

adapter_scale = 2.0
AXES = ("x", "zh", "c", "zl", "y")
SIZES = (4, 2, 2, 4, 4)
DIM = 512


def moves(target):
    pairs = []
    for source, place in enumerate(itertools.product(*[range(n) for n in SIZES])):
        index = 0
        for n, i in zip(SIZES, target(*place)):
            index = index * n + i % n
        pairs.append((source, index))
    return pairs


def send(value, target):
    return lax.ppermute(value, AXES, moves(target))


def after(value, *others):
    return lax.optimization_barrier((value, *others))[0]


def way(c):
    return 1 - 2 * c


def halved(value, bit, swap):
    rows = value.shape[0] // 2
    kept = lax.dynamic_slice_in_dim(value, bit * rows, rows)
    return kept + swap(lax.dynamic_slice_in_dim(value, (1 - bit) * rows, rows))


def doubled(value, bit, swap):
    there = swap(value)
    return jnp.where(
        bit == 0,
        jnp.concatenate([value, there], axis=0),
        jnp.concatenate([there, value], axis=0),
    )


def early_kernel(slot_ref, *refs):
    g_refs, w_refs = refs[:12], refs[12:20]
    w_out, acc_ref, gs, ws, g_sems, w_sems, out_sems = refs[20:]
    g_copies = [pltpu.make_async_copy(ref, gs.at[i], g_sems.at[i]) for i, ref in enumerate(g_refs)]
    for copy in g_copies:
        copy.start()
    for i in range(8):
        for s in range(2):
            slot = slot_ref[16 + 2 * i + s]
            pltpu.make_async_copy(
                w_refs[i].at[pl.ds(s * DIM, DIM)], ws.at[slot], w_sems.at[slot]
            ).start()
    acc_ref[...] = jnp.zeros_like(acc_ref)
    for copy in g_copies:
        copy.wait()

    def arrive(slot, carry):
        pltpu.make_async_copy(ws.at[slot], ws.at[slot], w_sems.at[slot]).wait()
        pltpu.make_async_copy(ws.at[slot], w_out.at[slot], out_sems.at[slot]).start()
        return carry

    lax.fori_loop(0, 16, arrive, 0)

    def step(i, carry):
        acc_ref[...] += lax.dot_general(
            gs[i],
            ws[slot_ref[i]],
            (((1,), (1,)), ((), ())),
            preferred_element_type=jnp.float32,
        )
        return carry

    lax.fori_loop(0, 12, step, 0)

    def leave(slot, carry):
        pltpu.make_async_copy(ws.at[slot], w_out.at[slot], out_sems.at[slot]).wait()
        return carry

    lax.fori_loop(0, 16, leave, 0)


def late_kernel(slot_ref, g0, g1, g2, g3, w_ref, acc_ref, add_ref, kept_ref, out_ref, gs, ws, g_sems, w_sems):
    copies = []
    for i, ref in enumerate((g0, g1, g2, g3)):
        g_copy = pltpu.make_async_copy(ref, gs.at[i], g_sems.at[i])
        w_copy = pltpu.make_async_copy(w_ref.at[slot_ref[12 + i]], ws.at[i], w_sems.at[i])
        g_copy.start()
        w_copy.start()
        copies += [g_copy, w_copy]
    for copy in copies:
        copy.wait()
    total = acc_ref[...]
    for i in range(4):
        total += lax.dot_general(gs[i], ws[i], (((1,), (1,)), ((), ())), preferred_element_type=jnp.float32)
    out_ref[...] = (total * kept_ref[...] + add_ref[...]).astype(out_ref.dtype)


def shards(projection_input, output_gradient, frozen_weight, down_adapters, up_adapters, lengths):
    tokens = output_gradient.shape[0]
    highest = lax.Precision.HIGHEST
    x, zh, c, zl, y = (lax.axis_index(a) for a in AXES)
    turn = way(c)

    positions = lax.iota(jnp.int32, tokens)
    kept = positions < lengths[0]
    masked_rows = output_gradient * kept.astype(output_gradient.dtype)[:, None]
    down_adapter = down_adapters[0]
    up_adapter = up_adapters[0]
    rank_width = down_adapter.shape[0]
    lowered_part = jnp.dot(projection_input, down_adapter.T, preferred_element_type=jnp.float32)
    pulled_part = jnp.dot(masked_rows, up_adapter.T, preferred_element_type=jnp.float32)
    rank_both = jnp.concatenate([lowered_part, pulled_part], axis=1)

    def place(s):
        return send(
            frozen_weight,
            lambda x, zh, c, zl, y: (zl + 2 * (y % 2), (y // 2) ^ s, y % 2, x, 2 * zh + c),
        )

    def along_x(held):
        return send(held, lambda x, zh, c, zl, y: (x + way(c), zh, c, zl, y))

    def to_sibling(held):
        return send(held, lambda x, zh, c, zl, y: (x, zh, 1 - c, zl, y))

    def along_z(here, j):
        return send(here, lambda x, zh, c, zl, y: (x, zh, c, zl + j, y))

    def onward(here):
        return send(here, lambda x, zh, c, zl, y: (x, zh, c, zl, y + way(c)))

    def backward(here):
        return send(here, lambda x, zh, c, zl, y: (x, zh, c, zl, y - way(c)))

    def in_rank(piece, dz, dy):
        return send(piece, lambda x, zh, c, zl, y: (x, zh, c, zl ^ dz, y ^ dy))

    placed = [place(0), place(1)]
    z1 = along_z(output_gradient, 1)
    behind_0, ahead_0 = onward(output_gradient), backward(output_gradient)
    across_0 = onward(behind_0)
    rank = halved(rank_both, (y & 1) ^ (y >> 1), lambda v: in_rank(v, 0, 1))
    own = [after(jnp.concatenate(placed, axis=0), ahead_0, across_0, z1, rank)]
    own.append(along_x(own[0]))
    z3 = along_z(after(output_gradient, z1, *placed), 3)
    behind_1, ahead_1 = onward(z1), backward(z1)
    rank = halved(rank, y >> 1, lambda v: in_rank(v, 0, 3))
    other = [to_sibling(own[0])]
    own.append(along_x(after(own[1], behind_1, ahead_1, z3, rank, other[0])))
    z2 = along_z(after(output_gradient, z3, own[1]), 2)
    across_1 = onward(behind_1)
    behind_3, ahead_3 = onward(z3), backward(z3)
    rank = rank + in_rank(rank, 1, 0)
    rank = rank + in_rank(rank, 2, 0)
    other.append(to_sibling(own[1]))
    own.append(along_x(after(own[2], behind_3, ahead_3, across_1, z2, rank, other[1])))
    behind_2, ahead_2 = onward(z2), backward(z2)
    across_3 = onward(behind_3)
    rank = doubled(rank, y >> 1, lambda v: in_rank(v, 0, 3))
    other.append(to_sibling(after(own[2], behind_2, ahead_2, across_3, rank)))
    other.append(to_sibling(own[3]))
    across_2 = onward(behind_2)
    rank_both = doubled(rank, (y & 1) ^ (y >> 1), lambda v: in_rank(v, 0, 1))
    first = [output_gradient, behind_0, ahead_0, across_0]
    second = [z1, behind_1, ahead_1, across_1, z3, behind_3, ahead_3, across_3]
    third = [z2, behind_2, ahead_2, across_2]

    places = [y, (y - turn) % 4, (y + turn) % 4, (y + 2) % 4]
    slots = [4 * ((zl - j) % 4) + place for j in (0, 1, 3, 2) for place in places]
    for core, direction in ((c, turn), (1 - c, -turn)):
        for t in range(4):
            for s in range(2):
                slots.append(4 * ((x - t * direction - 2 * core) % 4) + 2 * (zh ^ s) + core)
    slots = jnp.stack([jnp.asarray(v, jnp.int32) for v in slots])

    rank_projected = rank_both[:, :rank_width]
    scaled_gradient = adapter_scale * rank_both[:, rank_width:]
    adapter_part = jnp.dot(scaled_gradient, down_adapter.astype(jnp.float32), precision=highest)
    inverse_order = 1.0 / lengths[0].astype(jnp.float32)
    down_gradient = (
        jnp.dot(scaled_gradient.T, projection_input.astype(jnp.float32), precision=highest)
        * inverse_order
    )[None]
    up_gradient = (
        adapter_scale
        * jnp.dot(rank_projected.T, masked_rows.astype(jnp.float32), precision=highest)
        * inverse_order
    )[None]

    anywhere = pl.BlockSpec(memory_space=pl.ANY)
    in_vmem = pl.BlockSpec(memory_space=pltpu.VMEM)
    in_smem = pl.BlockSpec(memory_space=pltpu.SMEM)
    w_blocks, early = pl.pallas_call(
        early_kernel,
        out_shape=(
            jax.ShapeDtypeStruct((16, DIM, DIM), jnp.bfloat16),
            jax.ShapeDtypeStruct((tokens, DIM), jnp.float32),
        ),
        in_specs=[in_smem] + [anywhere] * 20,
        out_specs=(anywhere, in_vmem),
        scratch_shapes=[
            pltpu.VMEM((12, tokens, DIM), jnp.bfloat16),
            pltpu.VMEM((16, DIM, DIM), jnp.bfloat16),
            pltpu.SemaphoreType.DMA((12,)),
            pltpu.SemaphoreType.DMA((16,)),
            pltpu.SemaphoreType.DMA((16,)),
        ],
        compiler_params=pltpu.CompilerParams(vmem_limit_bytes=24 * 1024 * 1024),
        cost_estimate=pl.CostEstimate(
            flops=2 * tokens * DIM * DIM * 12, bytes_accessed=24 * 1024 * 1024, transcendentals=0
        ),
    )(slots, *first, *second, *own, *other)
    grad_input = pl.pallas_call(
        late_kernel,
        out_shape=jax.ShapeDtypeStruct((tokens, DIM), jnp.bfloat16),
        in_specs=[in_smem] + [anywhere] * 5 + [in_vmem] * 3,
        out_specs=in_vmem,
        scratch_shapes=[
            pltpu.VMEM((4, tokens, DIM), jnp.bfloat16),
            pltpu.VMEM((4, DIM, DIM), jnp.bfloat16),
            pltpu.SemaphoreType.DMA((4,)),
            pltpu.SemaphoreType.DMA((4,)),
        ],
        compiler_params=pltpu.CompilerParams(vmem_limit_bytes=24 * 1024 * 1024),
        cost_estimate=pl.CostEstimate(
            flops=2 * tokens * DIM * DIM * 4, bytes_accessed=6 * 1024 * 1024, transcendentals=0
        ),
    )(slots, *third, w_blocks, early, adapter_part, kept.astype(jnp.float32)[:, None])
    return (grad_input, down_gradient, up_gradient)


def solution(mesh):
    parts = Mesh(mesh.devices.reshape(SIZES), AXES)
    tenant, tensor = ("x", "zh", "c"), ("zl", "y")
    placed = (
        P(tenant, tensor),
        P(tenant, tensor),
        P(tenant, tensor),
        P(tenant, None, tensor),
        P(tenant, None, tensor),
        P(tenant),
    )
    return jax.shard_map(
        shards,
        mesh=parts,
        in_specs=placed,
        out_specs=(P(tenant, tensor), P(tenant, None, tensor), P(tenant, None, tensor)),
        check_vma=False,
    )
```

```python
import functools
import itertools

import jax
import jax.numpy as jnp
from jax import lax
from jax.experimental import pallas as pl
from jax.experimental.pallas import tpu as pltpu
from jax.sharding import Mesh, PartitionSpec as P

adapter_scale = 2.0
AXES = ("x", "zh", "c", "zl", "y")
SIZES = (4, 2, 2, 4, 4)
DIM = 512
VMEM = 56 * 1024 * 1024
ORDER = (
    "a A0 B0 Z1 Z3 Ry1:A0 | b0 b1 +Z A13 B13 Rz1 | +X XA XB Z2 +F F013 Ry3 | "
    "XF A2 B2 +S S1 Rz2 | F2 SF"
)
HELD = {"G": 0, "A0": 1, "B0": 1, "+Z": 1, "A13": 2, "B13": 2, "F013": 3, "Z2": 3, "A2": 4, "B2": 4, "F2": 5}
WEIGHTS = {"+X": 2, "XA": 3, "XB": 3, "S1": 4, "XF": 4, "SF": 5}
STAGES = (3, 4, 5)


def moves(target):
    pairs = []
    for source, place in enumerate(itertools.product(*[range(n) for n in SIZES])):
        index = 0
        for n, i in zip(SIZES, target(*place)):
            index = index * n + i % n
        pairs.append((source, index))
    return pairs


def send(value, target):
    return lax.ppermute(value, AXES, moves(target))


def after(value, *others):
    return lax.optimization_barrier((value, *others))[0]


def way(c):
    return 1 - 2 * c


def times(g, w):
    return lax.dot_general(g, w, (((1,), (1,)), ((), ())), preferred_element_type=jnp.float32)


def product_kernel(pairs, n_g, n_w, first, final, which_ref, *refs):
    g_refs, w_refs, rest = refs[:n_g], refs[n_g : n_g + n_w], refs[n_g + n_w :]
    if not first:
        sum_ref, rest = rest[0], rest[1:]
    if final:
        kept_ref, add_ref, rest = rest[0], rest[1], rest[2:]
    out_ref, gs, ws, acc, g_sems, w_sems = rest
    for k, (i, w_array, w_place, choices) in enumerate(pairs):
        for n, g_array, g_place in choices:

            @pl.when(which_ref[i] == n)
            def _():
                pltpu.make_async_copy(
                    g_refs[g_array].at[pl.ds(g_place * DIM, DIM)], gs.at[k], g_sems.at[k]
                ).start()
                pltpu.make_async_copy(
                    w_refs[w_array].at[pl.ds(w_place * DIM, DIM)], ws.at[k], w_sems.at[k]
                ).start()

    acc[...] = jnp.zeros_like(acc) if first else sum_ref[...]
    for k, (i, _, _, choices) in enumerate(pairs):
        hit = which_ref[i] == choices[0][0]
        for n, _, _ in choices[1:]:
            hit = jnp.logical_or(hit, which_ref[i] == n)

        @pl.when(hit)
        def _():
            pltpu.make_async_copy(gs.at[k], gs.at[k], g_sems.at[k]).wait()
            pltpu.make_async_copy(ws.at[k], ws.at[k], w_sems.at[k]).wait()
            acc[...] += times(gs[k], ws[k])

    if final:
        out_ref[...] = (acc[...] * kept_ref[...] + add_ref[...]).astype(out_ref.dtype)
    else:
        out_ref[...] = acc[...]


def partial_sum(stage, which, value, g_places, w_places, total, *ends):
    place = STAGES.index(stage)
    ahead = STAGES[place - 1] if place else -1
    g_names = [n for n in HELD if HELD[n] <= stage]
    w_names = [n for n in WEIGHTS if WEIGHTS[n] <= stage]
    pairs = []
    for i, (w_name, w_place) in enumerate(w_places):
        if w_name not in w_names:
            continue
        choices = [
            (n, g_name, g_place)
            for n, (g_name, g_place) in enumerate(g_places)
            if g_name in g_names and max(HELD[g_name], WEIGHTS[w_name]) > ahead
        ]
        if choices:
            pairs.append((i, w_name, w_place, choices))
    g_names = [n for n in g_names if any(g == n for p in pairs for _, g, _ in p[3])]
    w_names = [n for n in w_names if any(p[1] == n for p in pairs)]
    pairs = [
        (i, w_names.index(w), w_place, [(n, g_names.index(g), g_place) for n, g, g_place in choices])
        for i, w, w_place, choices in pairs
    ]
    rows = value["G"].shape[0]
    anywhere = pl.BlockSpec(memory_space=pl.ANY)
    in_vmem = pl.BlockSpec(memory_space=pltpu.VMEM)
    more = [v for v in (total, *ends) if v is not None]
    count = 16 if stage == STAGES[0] else 8
    return pl.pallas_call(
        functools.partial(product_kernel, pairs, len(g_names), len(w_names), total is None, bool(ends)),
        out_shape=jax.ShapeDtypeStruct((rows, DIM), jnp.bfloat16 if ends else jnp.float32),
        in_specs=[pl.BlockSpec(memory_space=pltpu.SMEM)]
        + [anywhere] * (len(g_names) + len(w_names))
        + [in_vmem] * len(more),
        out_specs=in_vmem,
        scratch_shapes=[
            pltpu.VMEM((len(pairs), rows, DIM), jnp.bfloat16),
            pltpu.VMEM((len(pairs), DIM, DIM), jnp.bfloat16),
            pltpu.VMEM((rows, DIM), jnp.float32),
            pltpu.SemaphoreType.DMA((len(pairs),)),
            pltpu.SemaphoreType.DMA((len(pairs),)),
        ],
        compiler_params=pltpu.CompilerParams(vmem_limit_bytes=VMEM),
        cost_estimate=pl.CostEstimate(
            flops=2 * rows * DIM * DIM * count,
            bytes_accessed=count * 1024 * 1024,
            transcendentals=0,
        ),
    )(which, *[value[n] for n in g_names], *[value[n] for n in w_names], *more)


def shards(projection_input, output_gradient, frozen_weight, down_adapters, up_adapters, lengths):
    tokens = output_gradient.shape[0]
    highest = lax.Precision.HIGHEST
    x, zh, c, zl, y = (lax.axis_index(a) for a in AXES)
    turn = way(c)

    positions = lax.iota(jnp.int32, tokens)
    kept = positions < lengths[0]
    masked_rows = output_gradient * kept.astype(output_gradient.dtype)[:, None]
    down_adapter = down_adapters[0]
    up_adapter = up_adapters[0]
    rank_width = down_adapter.shape[0]
    lowered_part = jnp.dot(projection_input, down_adapter.T, preferred_element_type=jnp.float32)
    pulled_part = jnp.dot(masked_rows, up_adapter.T, preferred_element_type=jnp.float32)
    rank_both = jnp.concatenate([lowered_part, pulled_part], axis=1)

    def to_half(s):
        return lambda x, zh, c, zl, y: (x, (y // 2) ^ s, c, zl + way(c) * x, 2 * zh + y % 2)

    def join(*parts):
        return jnp.concatenate(parts, axis=0)

    def swap(dz, dy):
        return lambda v: send(v, lambda x, zh, c, zl, y: (x, zh, c, zl ^ dz, y ^ dy))

    def add_from(dz, dy):
        return lambda v: v + swap(dz, dy)(v)

    def on(v):
        return send(v, lambda x, zh, c, zl, y: (x, zh, c, zl, y + way(c)))

    def back(v):
        return send(v, lambda x, zh, c, zl, y: (x, zh, c, zl, y - way(c)))

    def sibling(v):
        return send(v, lambda x, zh, c, zl, y: (x, zh, 1 - c, zl, y))

    steps = {
        "a": (("W",), lambda v: send(v, lambda x, zh, c, zl, y: (way(y % 2) * (x - zl), zh, y % 2, zl, 2 * (y // 2) + c))),
        "b0": (("a",), lambda v: send(v, to_half(0))),
        "b1": (("a",), lambda v: send(v, to_half(1))),
        "+X": (("b0", "b1"), join),
        "XA": (("+X",), lambda v: send(v, lambda x, zh, c, zl, y: (x + way(c), zh, c, zl, y))),
        "XB": (("+X",), lambda v: send(v, lambda x, zh, c, zl, y: (x - way(c), zh, c, zl, y))),
        "XF": (("XA",), lambda v: send(v, lambda x, zh, c, zl, y: (x + way(c), zh, c, zl, y))),
        "+S": (("+X", "XA", "XB"), join),
        "S1": (("+S",), sibling),
        "SF": (("XF",), sibling),
        "Z1": (("G",), lambda v: send(v, lambda x, zh, c, zl, y: (x, zh, c, zl + 1, y))),
        "Z2": (("G",), lambda v: send(v, lambda x, zh, c, zl, y: (x, zh, c, zl + 2, y))),
        "Z3": (("G",), lambda v: send(v, lambda x, zh, c, zl, y: (x, zh, c, zl + 3, y))),
        "+Z": (("Z1", "Z3"), join),
        "A0": (("G",), on),
        "B0": (("G",), back),
        "A13": (("+Z",), on),
        "B13": (("+Z",), back),
        "+F": (("A0", "A13"), join),
        "F013": (("+F",), on),
        "A2": (("Z2",), on),
        "B2": (("Z2",), back),
        "F2": (("A2",), on),
        "Ry1": (("R",), add_from(0, 1)),
        "Rz1": (("Ry1",), add_from(1, 0)),
        "Ry3": (("Rz1",), add_from(0, 3)),
        "Rz2": (("Ry3",), add_from(2, 0)),
    }
    value = {"W": frozen_weight, "G": output_gradient, "R": rank_both}
    g_places, g_slots = [], []
    for name in HELD:
        e = {"A": -turn, "B": turn, "F": 2}.get(name[0], 0)
        js = {"0": (0,), "G": (0,), "2": (2,)}.get(name[-1], (1, 3))
        js = (0, 1, 3) if name == "F013" else js
        for i, j in enumerate(js):
            g_places.append((name, i))
            g_slots.append(4 * ((zl - j) % 4) + (y + e) % 4)
    w_places, w_slots = [], []
    for name, core, froms in (
        ("+X", c, (x,)),
        ("XA", c, (x - turn,)),
        ("XB", c, (x + turn,)),
        ("S1", 1 - c, (x, x + turn, x - turn)),
        ("XF", c, (x + 2,)),
        ("SF", 1 - c, (x + 2,)),
    ):
        for i, from_x in enumerate(froms):
            for s in range(2):
                w_places.append((name, 2 * i + s))
                w_slots.append(4 * ((zl - way(core) * from_x) % 4) + 2 * (zh ^ s) + core)
    same = jnp.stack(w_slots)[:, None] == jnp.stack(g_slots)[None, :]
    which = jnp.sum(jnp.where(same, jnp.arange(16)[None, :], 0), axis=1).astype(jnp.int32)

    def ends(rank_both):
        rank_projected = rank_both[:, :rank_width]
        scaled_gradient = adapter_scale * rank_both[:, rank_width:]
        adapter_part = jnp.dot(scaled_gradient, down_adapter.astype(jnp.float32), precision=highest)
        inverse_order = 1.0 / lengths[0].astype(jnp.float32)
        down_gradient = (
            jnp.dot(scaled_gradient.T, projection_input.astype(jnp.float32), precision=highest)
            * inverse_order
        )[None]
        up_gradient = (
            adapter_scale
            * jnp.dot(rank_projected.T, masked_rows.astype(jnp.float32), precision=highest)
            * inverse_order
        )[None]
        return adapter_part, down_gradient, up_gradient

    before, beside = [], []
    for number, group in enumerate(ORDER.split("|"), 1):
        names = []
        for entry in group.split():
            name, mark, waits = entry.replace("=", ":=").partition(":")
            takes, act = steps[name]
            given = [value[n] for n in takes]
            if name[0] != "+":
                ahead = [] if waits[:1] == "=" else before
                ahead = ahead + [value[n] for n in waits.strip("=").split(",") if n]
                given[0] = after(given[0], *ahead) if ahead else given[0]
                names.append(name)
            value[name] = act(*given)
        before, beside = [value[n] for n in names] + beside, []
        if number == 3:
            total = partial_sum(number, which, value, g_places, w_places, None)
            beside = [total]
        if number == 4:
            total = partial_sum(number, which, value, g_places, w_places, total)
    adapter_part, down_gradient, up_gradient = ends(value["Rz2"])
    grad_input = partial_sum(5, which, value, g_places, w_places, total, kept.astype(jnp.float32)[:, None], adapter_part)
    return (grad_input, down_gradient, up_gradient)


def solution(mesh):
    parts = Mesh(mesh.devices.reshape(SIZES), AXES)
    tenant, tensor = ("x", "zh", "c"), ("zl", "y")
    placed = (
        P(tenant, tensor),
        P(tenant, tensor),
        P(tenant, tensor),
        P(tenant, None, tensor),
        P(tenant, None, tensor),
        P(tenant),
    )
    return jax.shard_map(
        shards,
        mesh=parts,
        in_specs=placed,
        out_specs=(P(tenant, tensor), P(tenant, None, tensor), P(tenant, None, tensor)),
        check_vma=False,
    )
```

```python
import functools
import itertools

import jax
import jax.numpy as jnp
from jax import lax
from jax.experimental import pallas as pl
from jax.experimental.pallas import tpu as pltpu
from jax.sharding import Mesh, PartitionSpec as P

adapter_scale = 2.0
AXES = ("x", "zh", "c", "zl", "y")
SIZES = (4, 2, 2, 4, 4)
DIM = 512
VMEM = 56 * 1024 * 1024
ORDER = (
    ("a", "A0", "B0", "Z1", "Z3", "Ry1:A0"),
    ("b0", "b1", "+Z", "A13", "B13", "Rz1"),
    ("+X", "XA", "XB", "Z2", "+F", "F013", "Ry3"),
    ("XF", "A2", "B2", "+S", "S1", "Rz2"),
    ("F2", "SF"),
)
HELD = {"G": 0, "A0": 1, "B0": 1, "+Z": 1, "A13": 2, "B13": 2, "F013": 3, "Z2": 3, "A2": 4, "B2": 4, "F2": 5}
WEIGHTS = {"+X": 2, "XA": 3, "XB": 3, "S1": 4, "XF": 4, "SF": 5}
STAGES = (3, 4, 5)


def moves(target):
    pairs = []
    for source, place in enumerate(itertools.product(*[range(n) for n in SIZES])):
        index = 0
        for n, i in zip(SIZES, target(*place)):
            index = index * n + i % n
        pairs.append((source, index))
    return pairs


def send(value, target):
    return lax.ppermute(value, AXES, moves(target))


def after(value, *others):
    return lax.optimization_barrier((value, *others))[0]


def way(c):
    return 1 - 2 * c


def times(g, w):
    return lax.dot_general(g, w, (((1,), (1,)), ((), ())), preferred_element_type=jnp.float32)


def product_kernel(pairs, n_g, n_w, first, final, which_ref, *refs):
    g_refs, w_refs, rest = refs[:n_g], refs[n_g : n_g + n_w], refs[n_g + n_w :]
    if not first:
        sum_ref, rest = rest[0], rest[1:]
    if final:
        kept_ref, add_ref, rest = rest[0], rest[1], rest[2:]
    out_ref, gs, ws, acc, g_sems, w_sems = rest
    for k, (i, w_array, w_place, choices) in enumerate(pairs):
        for n, g_array, g_place in choices:

            @pl.when(which_ref[i] == n)
            def _():
                pltpu.make_async_copy(
                    g_refs[g_array].at[pl.ds(g_place * DIM, DIM)], gs.at[k], g_sems.at[k]
                ).start()
                pltpu.make_async_copy(
                    w_refs[w_array].at[pl.ds(w_place * DIM, DIM)], ws.at[k], w_sems.at[k]
                ).start()

    acc[...] = jnp.zeros_like(acc) if first else sum_ref[...]
    for k, (i, _, _, choices) in enumerate(pairs):
        hit = which_ref[i] == choices[0][0]
        for n, _, _ in choices[1:]:
            hit = jnp.logical_or(hit, which_ref[i] == n)

        @pl.when(hit)
        def _():
            pltpu.make_async_copy(gs.at[k], gs.at[k], g_sems.at[k]).wait()
            pltpu.make_async_copy(ws.at[k], ws.at[k], w_sems.at[k]).wait()
            acc[...] += times(gs[k], ws[k])

    if final:
        out_ref[...] = (acc[...] * kept_ref[...] + add_ref[...]).astype(out_ref.dtype)
    else:
        out_ref[...] = acc[...]


def partial_sum(stage, which, value, g_places, w_places, total, *ends):
    place = STAGES.index(stage)
    ahead = STAGES[place - 1] if place else -1
    g_names = [n for n in HELD if HELD[n] <= stage]
    w_names = [n for n in WEIGHTS if WEIGHTS[n] <= stage]
    pairs = []
    for i, (w_name, w_place) in enumerate(w_places):
        if w_name not in w_names:
            continue
        choices = [
            (n, g_name, g_place)
            for n, (g_name, g_place) in enumerate(g_places)
            if g_name in g_names and max(HELD[g_name], WEIGHTS[w_name]) > ahead
        ]
        if choices:
            pairs.append((i, w_name, w_place, choices))
    g_names = [n for n in g_names if any(g == n for p in pairs for _, g, _ in p[3])]
    w_names = [n for n in w_names if any(p[1] == n for p in pairs)]
    pairs = [
        (i, w_names.index(w), w_place, [(n, g_names.index(g), g_place) for n, g, g_place in choices])
        for i, w, w_place, choices in pairs
    ]
    rows = value["G"].shape[0]
    anywhere = pl.BlockSpec(memory_space=pl.ANY)
    in_vmem = pl.BlockSpec(memory_space=pltpu.VMEM)
    more = [v for v in (total, *ends) if v is not None]
    count = 16 if stage == STAGES[0] else 8
    return pl.pallas_call(
        functools.partial(product_kernel, pairs, len(g_names), len(w_names), total is None, bool(ends)),
        out_shape=jax.ShapeDtypeStruct((rows, DIM), jnp.bfloat16 if ends else jnp.float32),
        in_specs=[pl.BlockSpec(memory_space=pltpu.SMEM)]
        + [anywhere] * (len(g_names) + len(w_names))
        + [in_vmem] * len(more),
        out_specs=in_vmem,
        scratch_shapes=[
            pltpu.VMEM((len(pairs), rows, DIM), jnp.bfloat16),
            pltpu.VMEM((len(pairs), DIM, DIM), jnp.bfloat16),
            pltpu.VMEM((rows, DIM), jnp.float32),
            pltpu.SemaphoreType.DMA((len(pairs),)),
            pltpu.SemaphoreType.DMA((len(pairs),)),
        ],
        compiler_params=pltpu.CompilerParams(vmem_limit_bytes=VMEM),
        cost_estimate=pl.CostEstimate(
            flops=2 * rows * DIM * DIM * count,
            bytes_accessed=count * 1024 * 1024,
            transcendentals=0,
        ),
    )(which, *[value[n] for n in g_names], *[value[n] for n in w_names], *more)


def shards(projection_input, output_gradient, frozen_weight, down_adapters, up_adapters, lengths):
    tokens = output_gradient.shape[0]
    highest = lax.Precision.HIGHEST
    x, zh, c, zl, y = (lax.axis_index(a) for a in AXES)
    turn = way(c)

    positions = lax.iota(jnp.int32, tokens)
    kept = positions < lengths[0]
    masked_rows = output_gradient * kept.astype(output_gradient.dtype)[:, None]
    down_adapter = down_adapters[0]
    up_adapter = up_adapters[0]
    rank_width = down_adapter.shape[0]
    lowered_part = jnp.dot(projection_input, down_adapter.T, preferred_element_type=jnp.float32)
    pulled_part = jnp.dot(masked_rows, up_adapter.T, preferred_element_type=jnp.float32)
    rank_both = jnp.concatenate([lowered_part, pulled_part], axis=1)

    def to_half(s):
        return lambda x, zh, c, zl, y: (x, (y // 2) ^ s, c, zl + way(c) * x, 2 * zh + y % 2)

    def join(*parts):
        return jnp.concatenate(parts, axis=0)

    def swap(dz, dy):
        return lambda v: send(v, lambda x, zh, c, zl, y: (x, zh, c, zl ^ dz, y ^ dy))

    def add_from(dz, dy):
        return lambda v: v + swap(dz, dy)(v)

    def on(v):
        return send(v, lambda x, zh, c, zl, y: (x, zh, c, zl, y + way(c)))

    def back(v):
        return send(v, lambda x, zh, c, zl, y: (x, zh, c, zl, y - way(c)))

    def sibling(v):
        return send(v, lambda x, zh, c, zl, y: (x, zh, 1 - c, zl, y))

    steps = {
        "a": (("W",), lambda v: send(v, lambda x, zh, c, zl, y: (way(y % 2) * (x - zl), zh, y % 2, zl, 2 * (y // 2) + c))),
        "b0": (("a",), lambda v: send(v, to_half(0))),
        "b1": (("a",), lambda v: send(v, to_half(1))),
        "+X": (("b0", "b1"), join),
        "XA": (("+X",), lambda v: send(v, lambda x, zh, c, zl, y: (x + way(c), zh, c, zl, y))),
        "XB": (("+X",), lambda v: send(v, lambda x, zh, c, zl, y: (x - way(c), zh, c, zl, y))),
        "XF": (("XA",), lambda v: send(v, lambda x, zh, c, zl, y: (x + way(c), zh, c, zl, y))),
        "+S": (("+X", "XA", "XB"), join),
        "S1": (("+S",), sibling),
        "SF": (("XF",), sibling),
        "Z1": (("G",), lambda v: send(v, lambda x, zh, c, zl, y: (x, zh, c, zl + 1, y))),
        "Z2": (("G",), lambda v: send(v, lambda x, zh, c, zl, y: (x, zh, c, zl + 2, y))),
        "Z3": (("G",), lambda v: send(v, lambda x, zh, c, zl, y: (x, zh, c, zl + 3, y))),
        "+Z": (("Z1", "Z3"), join),
        "A0": (("G",), on),
        "B0": (("G",), back),
        "A13": (("+Z",), on),
        "B13": (("+Z",), back),
        "+F": (("A0", "A13"), join),
        "F013": (("+F",), on),
        "A2": (("Z2",), on),
        "B2": (("Z2",), back),
        "F2": (("A2",), on),
        "Ry1": (("R",), add_from(0, 1)),
        "Rz1": (("Ry1",), add_from(1, 0)),
        "Ry3": (("Rz1",), add_from(0, 3)),
        "Rz2": (("Ry3",), add_from(2, 0)),
    }
    value = {"W": frozen_weight, "G": output_gradient, "R": rank_both}
    g_places, g_slots = [], []
    for name in HELD:
        e = {"A": -turn, "B": turn, "F": 2}.get(name[0], 0)
        js = {"0": (0,), "G": (0,), "2": (2,)}.get(name[-1], (1, 3))
        js = (0, 1, 3) if name == "F013" else js
        for i, j in enumerate(js):
            g_places.append((name, i))
            g_slots.append(4 * ((zl - j) % 4) + (y + e) % 4)
    w_places, w_slots = [], []
    for name, core, froms in (
        ("+X", c, (x,)),
        ("XA", c, (x - turn,)),
        ("XB", c, (x + turn,)),
        ("S1", 1 - c, (x, x + turn, x - turn)),
        ("XF", c, (x + 2,)),
        ("SF", 1 - c, (x + 2,)),
    ):
        for i, from_x in enumerate(froms):
            for s in range(2):
                w_places.append((name, 2 * i + s))
                w_slots.append(4 * ((zl - way(core) * from_x) % 4) + 2 * (zh ^ s) + core)
    same = jnp.stack(w_slots)[:, None] == jnp.stack(g_slots)[None, :]
    which = jnp.sum(jnp.where(same, jnp.arange(16)[None, :], 0), axis=1).astype(jnp.int32)

    def ends(rank_both):
        rank_projected = rank_both[:, :rank_width]
        scaled_gradient = adapter_scale * rank_both[:, rank_width:]
        adapter_part = jnp.dot(scaled_gradient, down_adapter.astype(jnp.float32), precision=highest)
        inverse_order = 1.0 / lengths[0].astype(jnp.float32)
        down_gradient = (
            jnp.dot(scaled_gradient.T, projection_input.astype(jnp.float32), precision=highest)
            * inverse_order
        )[None]
        up_gradient = (
            adapter_scale
            * jnp.dot(rank_projected.T, masked_rows.astype(jnp.float32), precision=highest)
            * inverse_order
        )[None]
        return adapter_part, down_gradient, up_gradient

    before, beside = [], []
    for number, group in enumerate(ORDER, 1):
        names = []
        for entry in group:
            name, _, waits = entry.partition(":")
            takes, act = steps[name]
            given = [value[n] for n in takes]
            if name[0] != "+":
                given[0] = after(given[0], *before, *[value[n] for n in waits.split(",") if n])
                names.append(name)
            value[name] = act(*given)
        before, beside = [value[n] for n in names] + beside, []
        if number == 3:
            total = partial_sum(number, which, value, g_places, w_places, None)
            beside = [total]
        if number == 4:
            total = partial_sum(number, which, value, g_places, w_places, total)
    adapter_part, down_gradient, up_gradient = ends(value["Rz2"])
    grad_input = partial_sum(5, which, value, g_places, w_places, total, kept.astype(jnp.float32)[:, None], adapter_part)
    return (grad_input, down_gradient, up_gradient)


def solution(mesh):
    parts = Mesh(mesh.devices.reshape(SIZES), AXES)
    tenant, tensor = ("x", "zh", "c"), ("zl", "y")
    placed = (
        P(tenant, tensor),
        P(tenant, tensor),
        P(tenant, tensor),
        P(tenant, None, tensor),
        P(tenant, None, tensor),
        P(tenant),
    )
    return jax.shard_map(
        shards,
        mesh=parts,
        in_specs=placed,
        out_specs=(P(tenant, tensor), P(tenant, None, tensor), P(tenant, None, tensor)),
        check_vma=False,
    )
```

```python
import functools
import itertools

import jax
import jax.numpy as jnp
from jax import lax
from jax.experimental import pallas as pl
from jax.experimental.pallas import tpu as pltpu
from jax.sharding import Mesh, PartitionSpec as P

adapter_scale = 2.0
AXES = ("x", "zh", "c", "zl", "y")
SIZES = (4, 2, 2, 4, 4)
DIM = 512
VMEM = 56 * 1024 * 1024
NEXT_VMEM = 46 * 1024 * 1024
LAST_VMEM = 16 * 1024 * 1024
ORDER = (
    ("a", "A0", "B0", "Z1", "Z3", "Ry1:A0"),
    ("b0", "b1", "+Z", "A13", "B13", "Rz1"),
    ("+X", "XA", "XB", "Z2", "+F", "F013", "Ry3"),
    ("XF", "A2", "B2", "+S", "S1", "Rz2"),
    ("F2", "SF"),
)
HELD = {"G": 0, "A0": 1, "B0": 1, "+Z": 1, "A13": 2, "B13": 2, "F013": 3, "Z2": 3, "A2": 4, "B2": 4, "F2": 5}
WEIGHTS = {"+X": 2, "XA": 3, "XB": 3, "S1": 4, "XF": 4, "SF": 5}
STAGES = (3, 4)


def moves(target):
    pairs = []
    for source, place in enumerate(itertools.product(*[range(n) for n in SIZES])):
        index = 0
        for n, i in zip(SIZES, target(*place)):
            index = index * n + i % n
        pairs.append((source, index))
    return pairs


def send(value, target):
    return lax.ppermute(value, AXES, moves(target))


def after(value, *others):
    return lax.optimization_barrier((value, *others))[0]


def way(c):
    return 1 - 2 * c


def times(g, w):
    return lax.dot_general(g, w, (((1,), (1,)), ((), ())), preferred_element_type=jnp.float32)


def product_kernel(pairs, aside, n_g, n_w, first, which_ref, *refs):
    g_refs, w_refs, rest = refs[:n_g], refs[n_g : n_g + n_w], refs[n_g + n_w :]
    if not first:
        sum_ref, rest = rest[0], rest[1:]
    out_ref, rest = rest[0], rest[1:]
    if aside:
        g_out, w_out, rest = rest[0], rest[1], rest[2:]
    gs, ws, acc, g_sems, w_sems, aside_sems = rest

    def block(ref, place):
        return ref.at[pl.ds(place * DIM, DIM)]

    for k, (i, w_array, w_place, choices) in enumerate(pairs):
        for n, g_array, g_place in choices:

            @pl.when(which_ref[i] == n)
            def _():
                pltpu.make_async_copy(block(g_refs[g_array], g_place), gs.at[k], g_sems.at[k]).start()
                pltpu.make_async_copy(block(w_refs[w_array], w_place), ws.at[k], w_sems.at[k]).start()

    if aside:
        for u in range(2):
            for n, g_array, g_place in aside:

                @pl.when(which_ref[14 + u] == n)
                def _():
                    pltpu.make_async_copy(block(g_refs[g_array], g_place), g_out.at[u], aside_sems.at[u]).start()

        for i, w_array, w_place, _ in pairs:

            @pl.when(which_ref[i] == 15)
            def _():
                pltpu.make_async_copy(block(w_refs[w_array], w_place), w_out, aside_sems.at[2]).start()

    acc[...] = jnp.zeros_like(acc) if first else sum_ref[...]
    for k, (i, _, _, choices) in enumerate(pairs):
        hit = which_ref[i] == choices[0][0]
        for n, _, _ in choices[1:]:
            hit = jnp.logical_or(hit, which_ref[i] == n)

        @pl.when(hit)
        def _():
            pltpu.make_async_copy(gs.at[k], gs.at[k], g_sems.at[k]).wait()
            pltpu.make_async_copy(ws.at[k], ws.at[k], w_sems.at[k]).wait()
            acc[...] += times(gs[k], ws[k])

    out_ref[...] = acc[...]
    if aside:
        for u in range(2):

            @pl.when(which_ref[14 + u] != 15)
            def _():
                pltpu.make_async_copy(g_out.at[u], g_out.at[u], aside_sems.at[u]).wait()

        @pl.when(jnp.logical_and(which_ref[14] != 15, which_ref[15] != 15))
        def _():
            pltpu.make_async_copy(w_out, w_out, aside_sems.at[2]).wait()


def last_kernel(which_ref, g_ref, w_ref, g_aside, w_aside, sum_ref, kept_ref, add_ref, out_ref, acc):
    acc[...] = sum_ref[...]
    for u in range(2):
        rows = slice(u * DIM, (u + 1) * DIM)

        @pl.when(which_ref[14 + u] == 15)
        def _():
            acc[...] += times(g_ref[...], w_ref[rows])

        @pl.when(which_ref[14 + u] != 15)
        def _():
            acc[...] += times(g_aside[u], w_ref[rows])

    @pl.when(jnp.logical_and(which_ref[14] != 15, which_ref[15] != 15))
    def _():
        acc[...] += times(g_ref[...], w_aside[...])

    out_ref[...] = (acc[...] * kept_ref[...] + add_ref[...]).astype(out_ref.dtype)


def costs(rows, count, vmem):
    return {
        "compiler_params": pltpu.CompilerParams(vmem_limit_bytes=vmem),
        "cost_estimate": pl.CostEstimate(
            flops=2 * rows * DIM * DIM * count,
            bytes_accessed=count * 1024 * 1024,
            transcendentals=0,
        ),
    }


def partial_sum(stage, which, value, g_places, w_places, total):
    first, aside = total is None, []
    ahead = -1 if first else STAGES[0]
    g_names = [n for n in HELD if HELD[n] <= stage]
    w_names = [n for n in WEIGHTS if WEIGHTS[n] <= stage]
    pairs = []
    for i, (w_name, w_place) in enumerate(w_places):
        if w_name not in w_names:
            continue
        choices = [
            (n, g_names.index(g_name), g_place)
            for n, (g_name, g_place) in enumerate(g_places)
            if g_name in g_names and max(HELD[g_name], WEIGHTS[w_name]) > ahead
        ]
        pairs.append((i, w_names.index(w_name), w_place, choices))
    if not first:
        aside = [(n, g_names.index(g), g_place) for n, (g, g_place) in enumerate(g_places) if g in g_names]
    rows = value["G"].shape[0]
    anywhere = pl.BlockSpec(memory_space=pl.ANY)
    in_vmem = pl.BlockSpec(memory_space=pltpu.VMEM)
    shapes = [jax.ShapeDtypeStruct((rows, DIM), jnp.float32)]
    if aside:
        shapes.append(jax.ShapeDtypeStruct((2, rows, DIM), jnp.bfloat16))
        shapes.append(jax.ShapeDtypeStruct((DIM, DIM), jnp.bfloat16))
    return pl.pallas_call(
        functools.partial(product_kernel, pairs, aside, len(g_names), len(w_names), first),
        out_shape=shapes,
        in_specs=[pl.BlockSpec(memory_space=pltpu.SMEM)]
        + [anywhere] * (len(g_names) + len(w_names))
        + ([] if first else [in_vmem]),
        out_specs=[in_vmem] * len(shapes),
        scratch_shapes=[
            pltpu.VMEM((len(pairs), rows, DIM), jnp.bfloat16),
            pltpu.VMEM((len(pairs), DIM, DIM), jnp.bfloat16),
            pltpu.VMEM((rows, DIM), jnp.float32),
            pltpu.SemaphoreType.DMA((len(pairs),)),
            pltpu.SemaphoreType.DMA((len(pairs),)),
            pltpu.SemaphoreType.DMA((3,)),
        ],
        **costs(rows, 16 if first else 8, VMEM if first else NEXT_VMEM),
    )(which, *[value[n] for n in g_names], *[value[n] for n in w_names], *([] if first else [total]))


def last_sum(which, *arrays):
    in_vmem = pl.BlockSpec(memory_space=pltpu.VMEM)
    rows = arrays[0].shape[0]
    return pl.pallas_call(
        last_kernel,
        out_shape=jax.ShapeDtypeStruct((rows, DIM), jnp.bfloat16),
        in_specs=[pl.BlockSpec(memory_space=pltpu.SMEM)] + [in_vmem] * len(arrays),
        out_specs=in_vmem,
        scratch_shapes=[pltpu.VMEM((rows, DIM), jnp.float32)],
        **costs(rows, 3, LAST_VMEM),
    )(which, *arrays)


def shards(projection_input, output_gradient, frozen_weight, down_adapters, up_adapters, lengths):
    tokens = output_gradient.shape[0]
    highest = lax.Precision.HIGHEST
    x, zh, c, zl, y = (lax.axis_index(a) for a in AXES)
    turn = way(c)

    positions = lax.iota(jnp.int32, tokens)
    kept = positions < lengths[0]
    masked_rows = output_gradient * kept.astype(output_gradient.dtype)[:, None]
    down_adapter = down_adapters[0]
    up_adapter = up_adapters[0]
    rank_width = down_adapter.shape[0]
    lowered_part = jnp.dot(projection_input, down_adapter.T, preferred_element_type=jnp.float32)
    pulled_part = jnp.dot(masked_rows, up_adapter.T, preferred_element_type=jnp.float32)
    rank_both = jnp.concatenate([lowered_part, pulled_part], axis=1)

    def to_half(s):
        return lambda x, zh, c, zl, y: (x, (y // 2) ^ s, c, zl + way(c) * x, 2 * zh + y % 2)

    def join(*parts):
        return jnp.concatenate(parts, axis=0)

    def swap(dz, dy):
        return lambda v: send(v, lambda x, zh, c, zl, y: (x, zh, c, zl ^ dz, y ^ dy))

    def add_from(dz, dy):
        return lambda v: v + swap(dz, dy)(v)

    def on(v):
        return send(v, lambda x, zh, c, zl, y: (x, zh, c, zl, y + way(c)))

    def back(v):
        return send(v, lambda x, zh, c, zl, y: (x, zh, c, zl, y - way(c)))

    def sibling(v):
        return send(v, lambda x, zh, c, zl, y: (x, zh, 1 - c, zl, y))

    steps = {
        "a": (("W",), lambda v: send(v, lambda x, zh, c, zl, y: (way(y % 2) * (x - zl), zh, y % 2, zl, 2 * (y // 2) + c))),
        "b0": (("a",), lambda v: send(v, to_half(0))),
        "b1": (("a",), lambda v: send(v, to_half(1))),
        "+X": (("b0", "b1"), join),
        "XA": (("+X",), lambda v: send(v, lambda x, zh, c, zl, y: (x + way(c), zh, c, zl, y))),
        "XB": (("+X",), lambda v: send(v, lambda x, zh, c, zl, y: (x - way(c), zh, c, zl, y))),
        "XF": (("XA",), lambda v: send(v, lambda x, zh, c, zl, y: (x + way(c), zh, c, zl, y))),
        "+S": (("+X", "XA", "XB"), join),
        "S1": (("+S",), sibling),
        "SF": (("XF",), sibling),
        "Z1": (("G",), lambda v: send(v, lambda x, zh, c, zl, y: (x, zh, c, zl + 1, y))),
        "Z2": (("G",), lambda v: send(v, lambda x, zh, c, zl, y: (x, zh, c, zl + 2, y))),
        "Z3": (("G",), lambda v: send(v, lambda x, zh, c, zl, y: (x, zh, c, zl + 3, y))),
        "+Z": (("Z1", "Z3"), join),
        "A0": (("G",), on),
        "B0": (("G",), back),
        "A13": (("+Z",), on),
        "B13": (("+Z",), back),
        "+F": (("A0", "A13"), join),
        "F013": (("+F",), on),
        "A2": (("Z2",), on),
        "B2": (("Z2",), back),
        "F2": (("A2",), on),
        "Ry1": (("R",), add_from(0, 1)),
        "Rz1": (("Ry1",), add_from(1, 0)),
        "Ry3": (("Rz1",), add_from(0, 3)),
        "Rz2": (("Ry3",), add_from(2, 0)),
    }
    value = {"W": frozen_weight, "G": output_gradient, "R": rank_both}
    g_places, g_slots = [], []
    for name in HELD:
        e = {"A": -turn, "B": turn, "F": 2}.get(name[0], 0)
        js = {"0": (0,), "G": (0,), "2": (2,)}.get(name[-1], (1, 3))
        js = (0, 1, 3) if name == "F013" else js
        for i, j in enumerate(js):
            g_places.append((name, i))
            g_slots.append(4 * ((zl - j) % 4) + (y + e) % 4)
    w_places, w_slots = [], []
    for name, core, froms in (
        ("+X", c, (x,)),
        ("XA", c, (x - turn,)),
        ("XB", c, (x + turn,)),
        ("S1", 1 - c, (x, x + turn, x - turn)),
        ("XF", c, (x + 2,)),
        ("SF", 1 - c, (x + 2,)),
    ):
        for i, from_x in enumerate(froms):
            for s in range(2):
                w_places.append((name, 2 * i + s))
                w_slots.append(4 * ((zl - way(core) * from_x) % 4) + 2 * (zh ^ s) + core)
    same = jnp.stack(w_slots)[:, None] == jnp.stack(g_slots)[None, :]
    which = jnp.sum(jnp.where(same, jnp.arange(16)[None, :], 0), axis=1).astype(jnp.int32)

    def ends(rank_both):
        rank_projected = rank_both[:, :rank_width]
        scaled_gradient = adapter_scale * rank_both[:, rank_width:]
        adapter_part = jnp.dot(scaled_gradient, down_adapter.astype(jnp.float32), precision=highest)
        inverse_order = 1.0 / lengths[0].astype(jnp.float32)
        down_gradient = (
            jnp.dot(scaled_gradient.T, projection_input.astype(jnp.float32), precision=highest)
            * inverse_order
        )[None]
        up_gradient = (
            adapter_scale
            * jnp.dot(rank_projected.T, masked_rows.astype(jnp.float32), precision=highest)
            * inverse_order
        )[None]
        return adapter_part, down_gradient, up_gradient

    before, beside = [], []
    for number, group in enumerate(ORDER, 1):
        names = []
        for entry in group:
            name, _, waits = entry.partition(":")
            takes, act = steps[name]
            given = [value[n] for n in takes]
            if name[0] != "+":
                given[0] = after(given[0], *before, *[value[n] for n in waits.split(",") if n])
                names.append(name)
            value[name] = act(*given)
        before, beside = [value[n] for n in names] + beside, []
        if number == 3:
            (total,) = partial_sum(number, which, value, g_places, w_places, None)
            beside = [total]
        if number == 4:
            total, g_aside, w_aside = partial_sum(number, which, value, g_places, w_places, total)
    adapter_part, down_gradient, up_gradient = ends(value["Rz2"])
    kept_column = kept.astype(jnp.float32)[:, None]
    grad_input = last_sum(which, value["F2"], value["SF"], g_aside, w_aside, total, kept_column, adapter_part)
    return (grad_input, down_gradient, up_gradient)


def solution(mesh):
    parts = Mesh(mesh.devices.reshape(SIZES), AXES)
    tenant, tensor = ("x", "zh", "c"), ("zl", "y")
    placed = (
        P(tenant, tensor),
        P(tenant, tensor),
        P(tenant, tensor),
        P(tenant, None, tensor),
        P(tenant, None, tensor),
        P(tenant),
    )
    return jax.shard_map(
        shards,
        mesh=parts,
        in_specs=placed,
        out_specs=(P(tenant, tensor), P(tenant, None, tensor), P(tenant, None, tensor)),
        check_vma=False,
    )
```

```python
import functools
import itertools

import jax
import jax.numpy as jnp
from jax import lax
from jax.experimental import pallas as pl
from jax.experimental.pallas import tpu as pltpu
from jax.sharding import Mesh, PartitionSpec as P

adapter_scale = 2.0
AXES = ("x", "zh", "c", "zl", "y")
SIZES = (4, 2, 2, 4, 4)
DIM = 512
VMEM = 56 * 1024 * 1024
NEXT_VMEM = 46 * 1024 * 1024
LAST_VMEM = 16 * 1024 * 1024
ORDER = (
    ("a", "A0", "B0", "Z1", "Z3", "Ry1:A0"),
    ("b0", "b1", "+Z", "A13", "B13", "Rz1"),
    ("+X", "XA", "XB", "Z2", "+F", "F013", "Ry3"),
    ("XF", "A2", "B2", "+S", "S1", "Rz2"),
    ("F2", "SF", "Ry4"),
)
HELD = {"G": 0, "A0": 1, "B0": 1, "+Z": 1, "A13": 2, "B13": 2, "F013": 3, "Z2": 3, "A2": 4, "B2": 4, "F2": 5}
WEIGHTS = {"+X": 2, "XA": 3, "XB": 3, "S1": 4, "XF": 4, "SF": 5}
STAGES = (3, 4)


def moves(target):
    pairs = []
    for source, place in enumerate(itertools.product(*[range(n) for n in SIZES])):
        index = 0
        for n, i in zip(SIZES, target(*place)):
            index = index * n + i % n
        pairs.append((source, index))
    return pairs


def send(value, target):
    return lax.ppermute(value, AXES, moves(target))


def after(value, *others):
    return lax.optimization_barrier((value, *others))[0]


def way(c):
    return 1 - 2 * c


def times(g, w):
    return lax.dot_general(g, w, (((1,), (1,)), ((), ())), preferred_element_type=jnp.float32)


def product_kernel(pairs, aside, n_g, n_w, first, which_ref, *refs):
    g_refs, w_refs, rest = refs[:n_g], refs[n_g : n_g + n_w], refs[n_g + n_w :]
    if not first:
        sum_ref, rest = rest[0], rest[1:]
    out_ref, rest = rest[0], rest[1:]
    if aside:
        g_out, w_out, rest = rest[0], rest[1], rest[2:]
    gs, ws, acc, g_sems, w_sems, aside_sems = rest

    def block(ref, place):
        return ref.at[pl.ds(place * DIM, DIM)]

    for k, (i, w_array, w_place, choices) in enumerate(pairs):
        for n, g_array, g_place in choices:

            @pl.when(which_ref[i] == n)
            def _():
                pltpu.make_async_copy(block(g_refs[g_array], g_place), gs.at[k], g_sems.at[k]).start()
                pltpu.make_async_copy(block(w_refs[w_array], w_place), ws.at[k], w_sems.at[k]).start()

    if aside:
        for u in range(2):
            for n, g_array, g_place in aside:

                @pl.when(which_ref[14 + u] == n)
                def _():
                    pltpu.make_async_copy(block(g_refs[g_array], g_place), g_out.at[u], aside_sems.at[u]).start()

        for i, w_array, w_place, _ in pairs:

            @pl.when(which_ref[i] == 15)
            def _():
                pltpu.make_async_copy(block(w_refs[w_array], w_place), w_out, aside_sems.at[2]).start()

    acc[...] = jnp.zeros_like(acc) if first else sum_ref[...]
    for k, (i, _, _, choices) in enumerate(pairs):
        hit = which_ref[i] == choices[0][0]
        for n, _, _ in choices[1:]:
            hit = jnp.logical_or(hit, which_ref[i] == n)

        @pl.when(hit)
        def _():
            pltpu.make_async_copy(gs.at[k], gs.at[k], g_sems.at[k]).wait()
            pltpu.make_async_copy(ws.at[k], ws.at[k], w_sems.at[k]).wait()
            acc[...] += times(gs[k], ws[k])

    out_ref[...] = acc[...]
    if aside:
        for u in range(2):

            @pl.when(which_ref[14 + u] != 15)
            def _():
                pltpu.make_async_copy(g_out.at[u], g_out.at[u], aside_sems.at[u]).wait()

        @pl.when(jnp.logical_and(which_ref[14] != 15, which_ref[15] != 15))
        def _():
            pltpu.make_async_copy(w_out, w_out, aside_sems.at[2]).wait()


def last_kernel(which_ref, g_ref, w_ref, g_aside, w_aside, sum_ref, kept_ref, add_ref, out_ref, acc):
    acc[...] = sum_ref[...]
    for u in range(2):
        rows = slice(u * DIM, (u + 1) * DIM)

        @pl.when(which_ref[14 + u] == 15)
        def _():
            acc[...] += times(g_ref[...], w_ref[rows])

        @pl.when(which_ref[14 + u] != 15)
        def _():
            acc[...] += times(g_aside[u], w_ref[rows])

    @pl.when(jnp.logical_and(which_ref[14] != 15, which_ref[15] != 15))
    def _():
        acc[...] += times(g_ref[...], w_aside[...])

    out_ref[...] = (acc[...] * kept_ref[...] + add_ref[...]).astype(out_ref.dtype)


def costs(rows, count, vmem):
    return {
        "compiler_params": pltpu.CompilerParams(vmem_limit_bytes=vmem),
        "cost_estimate": pl.CostEstimate(
            flops=2 * rows * DIM * DIM * count,
            bytes_accessed=count * 1024 * 1024,
            transcendentals=0,
        ),
    }


def partial_sum(stage, which, value, g_places, w_places, total):
    first, aside = total is None, []
    ahead = -1 if first else STAGES[0]
    g_names = [n for n in HELD if HELD[n] <= stage]
    w_names = [n for n in WEIGHTS if WEIGHTS[n] <= stage]
    pairs = []
    for i, (w_name, w_place) in enumerate(w_places):
        if w_name not in w_names:
            continue
        choices = [
            (n, g_names.index(g_name), g_place)
            for n, (g_name, g_place) in enumerate(g_places)
            if g_name in g_names and max(HELD[g_name], WEIGHTS[w_name]) > ahead
        ]
        pairs.append((i, w_names.index(w_name), w_place, choices))
    if not first:
        aside = [(n, g_names.index(g), g_place) for n, (g, g_place) in enumerate(g_places) if g in g_names]
    rows = value["G"].shape[0]
    anywhere = pl.BlockSpec(memory_space=pl.ANY)
    in_vmem = pl.BlockSpec(memory_space=pltpu.VMEM)
    shapes = [jax.ShapeDtypeStruct((rows, DIM), jnp.float32)]
    if aside:
        shapes.append(jax.ShapeDtypeStruct((2, rows, DIM), jnp.bfloat16))
        shapes.append(jax.ShapeDtypeStruct((DIM, DIM), jnp.bfloat16))
    return pl.pallas_call(
        functools.partial(product_kernel, pairs, aside, len(g_names), len(w_names), first),
        out_shape=shapes,
        in_specs=[pl.BlockSpec(memory_space=pltpu.SMEM)]
        + [anywhere] * (len(g_names) + len(w_names))
        + ([] if first else [in_vmem]),
        out_specs=[in_vmem] * len(shapes),
        scratch_shapes=[
            pltpu.VMEM((len(pairs), rows, DIM), jnp.bfloat16),
            pltpu.VMEM((len(pairs), DIM, DIM), jnp.bfloat16),
            pltpu.VMEM((rows, DIM), jnp.float32),
            pltpu.SemaphoreType.DMA((len(pairs),)),
            pltpu.SemaphoreType.DMA((len(pairs),)),
            pltpu.SemaphoreType.DMA((3,)),
        ],
        **costs(rows, 16 if first else 8, VMEM if first else NEXT_VMEM),
    )(which, *[value[n] for n in g_names], *[value[n] for n in w_names], *([] if first else [total]))


def last_sum(which, *arrays):
    in_vmem = pl.BlockSpec(memory_space=pltpu.VMEM)
    rows = arrays[0].shape[0]
    return pl.pallas_call(
        last_kernel,
        out_shape=jax.ShapeDtypeStruct((rows, DIM), jnp.bfloat16),
        in_specs=[pl.BlockSpec(memory_space=pltpu.SMEM)] + [in_vmem] * len(arrays),
        out_specs=in_vmem,
        scratch_shapes=[pltpu.VMEM((rows, DIM), jnp.float32)],
        **costs(rows, 3, LAST_VMEM),
    )(which, *arrays)


def shards(projection_input, output_gradient, frozen_weight, down_adapters, up_adapters, lengths):
    tokens = output_gradient.shape[0]
    highest = lax.Precision.HIGHEST
    x, zh, c, zl, y = (lax.axis_index(a) for a in AXES)
    turn = way(c)

    positions = lax.iota(jnp.int32, tokens)
    kept = positions < lengths[0]
    masked_rows = output_gradient * kept.astype(output_gradient.dtype)[:, None]
    down_adapter = down_adapters[0]
    up_adapter = up_adapters[0]
    rank_width = down_adapter.shape[0]
    lowered_part = jnp.dot(projection_input, down_adapter.T, preferred_element_type=jnp.float32)
    pulled_part = jnp.dot(masked_rows, up_adapter.T, preferred_element_type=jnp.float32)
    rank_both = jnp.concatenate([lowered_part, pulled_part], axis=1)

    def to_half(s):
        return lambda x, zh, c, zl, y: (x, (y // 2) ^ s, c, zl + way(c) * x, 2 * zh + y % 2)

    def join(*parts):
        return jnp.concatenate(parts, axis=0)

    def swap(dz, dy):
        return lambda v: send(v, lambda x, zh, c, zl, y: (x, zh, c, zl ^ dz, y ^ dy))

    def add_from(dz, dy):
        return lambda v: v + swap(dz, dy)(v)

    half = (y & 1) ^ (y >> 1)

    def halved(v):
        n = v.shape[0] // 2
        rest = swap(0, 1)(lax.dynamic_slice_in_dim(v, (1 - half) * n, n))
        return lax.dynamic_slice_in_dim(v, half * n, n) + rest

    def doubled(v):
        there = swap(0, 1)(v)
        return jnp.where(half == 0, join(v, there), join(there, v))

    def on(v):
        return send(v, lambda x, zh, c, zl, y: (x, zh, c, zl, y + way(c)))

    def back(v):
        return send(v, lambda x, zh, c, zl, y: (x, zh, c, zl, y - way(c)))

    def sibling(v):
        return send(v, lambda x, zh, c, zl, y: (x, zh, 1 - c, zl, y))

    steps = {
        "a": (("W",), lambda v: send(v, lambda x, zh, c, zl, y: (way(y % 2) * (x - zl), zh, y % 2, zl, 2 * (y // 2) + c))),
        "b0": (("a",), lambda v: send(v, to_half(0))),
        "b1": (("a",), lambda v: send(v, to_half(1))),
        "+X": (("b0", "b1"), join),
        "XA": (("+X",), lambda v: send(v, lambda x, zh, c, zl, y: (x + way(c), zh, c, zl, y))),
        "XB": (("+X",), lambda v: send(v, lambda x, zh, c, zl, y: (x - way(c), zh, c, zl, y))),
        "XF": (("XA",), lambda v: send(v, lambda x, zh, c, zl, y: (x + way(c), zh, c, zl, y))),
        "+S": (("+X", "XA", "XB"), join),
        "S1": (("+S",), sibling),
        "SF": (("XF",), sibling),
        "Z1": (("G",), lambda v: send(v, lambda x, zh, c, zl, y: (x, zh, c, zl + 1, y))),
        "Z2": (("G",), lambda v: send(v, lambda x, zh, c, zl, y: (x, zh, c, zl + 2, y))),
        "Z3": (("G",), lambda v: send(v, lambda x, zh, c, zl, y: (x, zh, c, zl + 3, y))),
        "+Z": (("Z1", "Z3"), join),
        "A0": (("G",), on),
        "B0": (("G",), back),
        "A13": (("+Z",), on),
        "B13": (("+Z",), back),
        "+F": (("A0", "A13"), join),
        "F013": (("+F",), on),
        "A2": (("Z2",), on),
        "B2": (("Z2",), back),
        "F2": (("A2",), on),
        "Ry1": (("R",), halved),
        "Rz1": (("Ry1",), add_from(1, 0)),
        "Ry3": (("Rz1",), add_from(0, 3)),
        "Rz2": (("Ry3",), add_from(2, 0)),
        "Ry4": (("Rz2",), doubled),
    }
    value = {"W": frozen_weight, "G": output_gradient, "R": rank_both}
    g_places, g_slots = [], []
    for name in HELD:
        e = {"A": -turn, "B": turn, "F": 2}.get(name[0], 0)
        js = {"0": (0,), "G": (0,), "2": (2,)}.get(name[-1], (1, 3))
        js = (0, 1, 3) if name == "F013" else js
        for i, j in enumerate(js):
            g_places.append((name, i))
            g_slots.append(4 * ((zl - j) % 4) + (y + e) % 4)
    w_places, w_slots = [], []
    for name, core, froms in (
        ("+X", c, (x,)),
        ("XA", c, (x - turn,)),
        ("XB", c, (x + turn,)),
        ("S1", 1 - c, (x, x + turn, x - turn)),
        ("XF", c, (x + 2,)),
        ("SF", 1 - c, (x + 2,)),
    ):
        for i, from_x in enumerate(froms):
            for s in range(2):
                w_places.append((name, 2 * i + s))
                w_slots.append(4 * ((zl - way(core) * from_x) % 4) + 2 * (zh ^ s) + core)
    same = jnp.stack(w_slots)[:, None] == jnp.stack(g_slots)[None, :]
    which = jnp.sum(jnp.where(same, jnp.arange(16)[None, :], 0), axis=1).astype(jnp.int32)

    def ends(rank_both):
        rank_projected = rank_both[:, :rank_width]
        scaled_gradient = adapter_scale * rank_both[:, rank_width:]
        adapter_part = jnp.dot(scaled_gradient, down_adapter.astype(jnp.float32), precision=highest)
        inverse_order = 1.0 / lengths[0].astype(jnp.float32)
        down_gradient = (
            jnp.dot(scaled_gradient.T, projection_input.astype(jnp.float32), precision=highest)
            * inverse_order
        )[None]
        up_gradient = (
            adapter_scale
            * jnp.dot(rank_projected.T, masked_rows.astype(jnp.float32), precision=highest)
            * inverse_order
        )[None]
        return adapter_part, down_gradient, up_gradient

    before, beside = [], []
    for number, group in enumerate(ORDER, 1):
        names = []
        for entry in group:
            name, _, waits = entry.partition(":")
            takes, act = steps[name]
            given = [value[n] for n in takes]
            if name[0] != "+":
                given[0] = after(given[0], *before, *[value[n] for n in waits.split(",") if n])
                names.append(name)
            value[name] = act(*given)
        before, beside = [value[n] for n in names] + beside, []
        if number == 3:
            (total,) = partial_sum(number, which, value, g_places, w_places, None)
            beside = [total]
        if number == 4:
            total, g_aside, w_aside = partial_sum(number, which, value, g_places, w_places, total)
    adapter_part, down_gradient, up_gradient = ends(value["Ry4"])
    kept_column = kept.astype(jnp.float32)[:, None]
    grad_input = last_sum(which, value["F2"], value["SF"], g_aside, w_aside, total, kept_column, adapter_part)
    return (grad_input, down_gradient, up_gradient)


def solution(mesh):
    parts = Mesh(mesh.devices.reshape(SIZES), AXES)
    tenant, tensor = ("x", "zh", "c"), ("zl", "y")
    placed = (
        P(tenant, tensor),
        P(tenant, tensor),
        P(tenant, tensor),
        P(tenant, None, tensor),
        P(tenant, None, tensor),
        P(tenant),
    )
    return jax.shard_map(
        shards,
        mesh=parts,
        in_specs=placed,
        out_specs=(P(tenant, tensor), P(tenant, None, tensor), P(tenant, None, tensor)),
        check_vma=False,
    )
```

```python
import functools
import itertools

import jax
import jax.numpy as jnp
from jax import lax
from jax.experimental import pallas as pl
from jax.experimental.pallas import tpu as pltpu
from jax.sharding import Mesh, PartitionSpec as P

adapter_scale = 2.0
AXES = ("x", "zh", "c", "zl", "y")
SIZES = (4, 2, 2, 4, 4)
DIM = 512
VMEM = 56 * 1024 * 1024
NEXT_VMEM = 46 * 1024 * 1024
LAST_VMEM = 16 * 1024 * 1024
ORDER = (
    ("a", "A0", "B0", "Z1", "Z3", "Ry1:A0"),
    ("b0", "b1", "+Z", "A13", "B13", "Rz1"),
    ("+X", "XA", "XB", "Z2", "+F", "F013", "Ry3"),
    ("XF", "A2", "B2", "+S", "S1", "Rz2"),
    ("F2", "SF", "Ry4"),
)
HELD = {"G": 0, "A0": 1, "B0": 1, "+Z": 1, "A13": 2, "B13": 2, "F013": 3, "Z2": 3, "A2": 4, "B2": 4, "F2": 5}
WEIGHTS = {"+X": 2, "XA": 3, "XB": 3, "S1": 4, "XF": 4, "SF": 5}
STAGES = (3, 4)


def moves(target):
    pairs = []
    for source, place in enumerate(itertools.product(*[range(n) for n in SIZES])):
        index = 0
        for n, i in zip(SIZES, target(*place)):
            index = index * n + i % n
        pairs.append((source, index))
    return pairs


def send(value, target):
    return lax.ppermute(value, AXES, moves(target))


def after(value, *others):
    return lax.optimization_barrier((value, *others))[0]


def way(c):
    return 1 - 2 * c


def times(g, w):
    return lax.dot_general(g, w, (((1,), (1,)), ((), ())), preferred_element_type=jnp.float32)


def product_kernel(pairs, aside, n_g, n_w, first, which_ref, *refs):
    g_refs, w_refs, rest = refs[:n_g], refs[n_g : n_g + n_w], refs[n_g + n_w :]
    if not first:
        sum_ref, rest = rest[0], rest[1:]
    out_ref, rest = rest[0], rest[1:]
    if aside:
        g_out, w_out, rest = rest[0], rest[1], rest[2:]
    gs, ws, acc, g_sems, w_sems, aside_sems = rest

    def block(ref, place):
        return ref.at[pl.ds(place * DIM, DIM)]

    for k, (i, w_array, w_place, choices) in enumerate(pairs):
        for n, g_array, g_place in choices:

            @pl.when(which_ref[i] == n)
            def _():
                pltpu.make_async_copy(block(g_refs[g_array], g_place), gs.at[k], g_sems.at[k]).start()
                pltpu.make_async_copy(block(w_refs[w_array], w_place), ws.at[k], w_sems.at[k]).start()

    if aside:
        for u in range(2):
            for n, g_array, g_place in aside:

                @pl.when(which_ref[14 + u] == n)
                def _():
                    pltpu.make_async_copy(block(g_refs[g_array], g_place), g_out.at[u], aside_sems.at[u]).start()

        for i, w_array, w_place, _ in pairs:

            @pl.when(which_ref[i] == 15)
            def _():
                pltpu.make_async_copy(block(w_refs[w_array], w_place), w_out, aside_sems.at[2]).start()

    acc[...] = jnp.zeros_like(acc) if first else sum_ref[...]
    for k, (i, _, _, choices) in enumerate(pairs):
        hit = which_ref[i] == choices[0][0]
        for n, _, _ in choices[1:]:
            hit = jnp.logical_or(hit, which_ref[i] == n)

        @pl.when(hit)
        def _():
            pltpu.make_async_copy(gs.at[k], gs.at[k], g_sems.at[k]).wait()
            pltpu.make_async_copy(ws.at[k], ws.at[k], w_sems.at[k]).wait()
            acc[...] += times(gs[k], ws[k])

    out_ref[...] = acc[...]
    if aside:
        for u in range(2):

            @pl.when(which_ref[14 + u] != 15)
            def _():
                pltpu.make_async_copy(g_out.at[u], g_out.at[u], aside_sems.at[u]).wait()

        @pl.when(jnp.logical_and(which_ref[14] != 15, which_ref[15] != 15))
        def _():
            pltpu.make_async_copy(w_out, w_out, aside_sems.at[2]).wait()


def last_kernel(which_ref, g_ref, w_ref, g_aside, w_aside, sum_ref, kept_ref, add_ref, out_ref, acc):
    acc[...] = sum_ref[...]
    for u in range(2):
        rows = slice(u * DIM, (u + 1) * DIM)

        @pl.when(which_ref[14 + u] == 15)
        def _():
            acc[...] += times(g_ref[...], w_ref[rows])

        @pl.when(which_ref[14 + u] != 15)
        def _():
            acc[...] += times(g_aside[u], w_ref[rows])

    @pl.when(jnp.logical_and(which_ref[14] != 15, which_ref[15] != 15))
    def _():
        acc[...] += times(g_ref[...], w_aside[...])

    out_ref[...] = (acc[...] * kept_ref[...] + add_ref[...]).astype(out_ref.dtype)


def costs(rows, count, vmem):
    return {
        "compiler_params": pltpu.CompilerParams(vmem_limit_bytes=vmem),
        "cost_estimate": pl.CostEstimate(
            flops=2 * rows * DIM * DIM * count,
            bytes_accessed=count * 1024 * 1024,
            transcendentals=0,
        ),
    }


def partial_sum(stage, which, value, g_places, w_places, total):
    first, aside = total is None, []
    ahead = -1 if first else STAGES[0]
    g_names = [n for n in HELD if HELD[n] <= stage]
    w_names = [n for n in WEIGHTS if WEIGHTS[n] <= stage]
    pairs = []
    for i, (w_name, w_place) in enumerate(w_places):
        if w_name not in w_names:
            continue
        choices = [
            (n, g_names.index(g_name), g_place)
            for n, (g_name, g_place) in enumerate(g_places)
            if g_name in g_names and max(HELD[g_name], WEIGHTS[w_name]) > ahead
        ]
        pairs.append((i, w_names.index(w_name), w_place, choices))
    if not first:
        aside = [(n, g_names.index(g), g_place) for n, (g, g_place) in enumerate(g_places) if g in g_names]
    rows = value["G"].shape[0]
    anywhere = pl.BlockSpec(memory_space=pl.ANY)
    in_vmem = pl.BlockSpec(memory_space=pltpu.VMEM)
    shapes = [jax.ShapeDtypeStruct((rows, DIM), jnp.float32)]
    if aside:
        shapes.append(jax.ShapeDtypeStruct((2, rows, DIM), jnp.bfloat16))
        shapes.append(jax.ShapeDtypeStruct((DIM, DIM), jnp.bfloat16))
    return pl.pallas_call(
        functools.partial(product_kernel, pairs, aside, len(g_names), len(w_names), first),
        out_shape=shapes,
        in_specs=[pl.BlockSpec(memory_space=pltpu.SMEM)]
        + [anywhere] * (len(g_names) + len(w_names))
        + ([] if first else [in_vmem]),
        out_specs=[in_vmem] * len(shapes),
        scratch_shapes=[
            pltpu.VMEM((len(pairs), rows, DIM), jnp.bfloat16),
            pltpu.VMEM((len(pairs), DIM, DIM), jnp.bfloat16),
            pltpu.VMEM((rows, DIM), jnp.float32),
            pltpu.SemaphoreType.DMA((len(pairs),)),
            pltpu.SemaphoreType.DMA((len(pairs),)),
            pltpu.SemaphoreType.DMA((3,)),
        ],
        **costs(rows, 16 if first else 8, VMEM if first else NEXT_VMEM),
    )(which, *[value[n] for n in g_names], *[value[n] for n in w_names], *([] if first else [total]))


def last_sum(which, *arrays):
    in_vmem = pl.BlockSpec(memory_space=pltpu.VMEM)
    rows = arrays[0].shape[0]
    return pl.pallas_call(
        last_kernel,
        out_shape=jax.ShapeDtypeStruct((rows, DIM), jnp.bfloat16),
        in_specs=[pl.BlockSpec(memory_space=pltpu.SMEM)] + [in_vmem] * len(arrays),
        out_specs=in_vmem,
        scratch_shapes=[pltpu.VMEM((rows, DIM), jnp.float32)],
        **costs(rows, 3, LAST_VMEM),
    )(which, *arrays)


def shards(projection_input, output_gradient, frozen_weight, down_adapters, up_adapters, lengths):
    tokens = output_gradient.shape[0]
    highest = lax.Precision.HIGHEST
    x, zh, c, zl, y = (lax.axis_index(a) for a in AXES)
    turn = way(c)

    positions = lax.iota(jnp.int32, tokens)
    kept = positions < lengths[0]
    masked_rows = output_gradient * kept.astype(output_gradient.dtype)[:, None]
    down_adapter = down_adapters[0]
    up_adapter = up_adapters[0]
    rank_width = down_adapter.shape[0]
    lowered_part = jnp.dot(projection_input, down_adapter.T, preferred_element_type=jnp.float32)
    pulled_part = jnp.dot(masked_rows, up_adapter.T, preferred_element_type=jnp.float32)
    rank_both = jnp.concatenate([lowered_part, pulled_part], axis=1)

    def to_half(s):
        return lambda x, zh, c, zl, y: (x, (y // 2) ^ s, c, zl + way(c) * x, 2 * zh + y % 2)

    def join(*parts):
        return jnp.concatenate(parts, axis=0)

    def in_turn(*parts):
        whole = jnp.zeros((sum(p.shape[0] for p in parts), parts[0].shape[1]), parts[0].dtype)
        for i, part in enumerate(parts):
            whole = lax.dynamic_update_slice(whole, part, (i * part.shape[0], 0))
        return whole

    def swap(dz, dy):
        return lambda v: send(v, lambda x, zh, c, zl, y: (x, zh, c, zl ^ dz, y ^ dy))

    def add_from(dz, dy):
        return lambda v: v + swap(dz, dy)(v)

    half = (y & 1) ^ (y >> 1)

    def halved(v):
        n = v.shape[0] // 2
        rest = swap(0, 1)(lax.dynamic_slice_in_dim(v, (1 - half) * n, n))
        return lax.dynamic_slice_in_dim(v, half * n, n) + rest

    def doubled(v):
        there = swap(0, 1)(v)
        return jnp.where(half == 0, join(v, there), join(there, v))

    def on(v):
        return send(v, lambda x, zh, c, zl, y: (x, zh, c, zl, y + way(c)))

    def back(v):
        return send(v, lambda x, zh, c, zl, y: (x, zh, c, zl, y - way(c)))

    def sibling(v):
        return send(v, lambda x, zh, c, zl, y: (x, zh, 1 - c, zl, y))

    steps = {
        "a": (("W",), lambda v: send(v, lambda x, zh, c, zl, y: (way(y % 2) * (x - zl), zh, y % 2, zl, 2 * (y // 2) + c))),
        "b0": (("a",), lambda v: send(v, to_half(0))),
        "b1": (("a",), lambda v: send(v, to_half(1))),
        "+X": (("b0", "b1"), join),
        "XA": (("+X",), lambda v: send(v, lambda x, zh, c, zl, y: (x + way(c), zh, c, zl, y))),
        "XB": (("+X",), lambda v: send(v, lambda x, zh, c, zl, y: (x - way(c), zh, c, zl, y))),
        "XF": (("XA",), lambda v: send(v, lambda x, zh, c, zl, y: (x + way(c), zh, c, zl, y))),
        "+S": (("+X", "XA", "XB"), in_turn),
        "S1": (("+S",), sibling),
        "SF": (("XF",), sibling),
        "Z1": (("G",), lambda v: send(v, lambda x, zh, c, zl, y: (x, zh, c, zl + 1, y))),
        "Z2": (("G",), lambda v: send(v, lambda x, zh, c, zl, y: (x, zh, c, zl + 2, y))),
        "Z3": (("G",), lambda v: send(v, lambda x, zh, c, zl, y: (x, zh, c, zl + 3, y))),
        "+Z": (("Z1", "Z3"), join),
        "A0": (("G",), on),
        "B0": (("G",), back),
        "A13": (("+Z",), on),
        "B13": (("+Z",), back),
        "+F": (("A0", "A13"), join),
        "F013": (("+F",), on),
        "A2": (("Z2",), on),
        "B2": (("Z2",), back),
        "F2": (("A2",), on),
        "Ry1": (("R",), halved),
        "Rz1": (("Ry1",), add_from(1, 0)),
        "Ry3": (("Rz1",), add_from(0, 3)),
        "Rz2": (("Ry3",), add_from(2, 0)),
        "Ry4": (("Rz2",), doubled),
    }
    value = {"W": frozen_weight, "G": output_gradient, "R": rank_both}
    g_places, g_slots = [], []
    for name in HELD:
        e = {"A": -turn, "B": turn, "F": 2}.get(name[0], 0)
        js = {"0": (0,), "G": (0,), "2": (2,)}.get(name[-1], (1, 3))
        js = (0, 1, 3) if name == "F013" else js
        for i, j in enumerate(js):
            g_places.append((name, i))
            g_slots.append(4 * ((zl - j) % 4) + (y + e) % 4)
    w_places, w_slots = [], []
    for name, core, froms in (
        ("+X", c, (x,)),
        ("XA", c, (x - turn,)),
        ("XB", c, (x + turn,)),
        ("S1", 1 - c, (x, x + turn, x - turn)),
        ("XF", c, (x + 2,)),
        ("SF", 1 - c, (x + 2,)),
    ):
        for i, from_x in enumerate(froms):
            for s in range(2):
                w_places.append((name, 2 * i + s))
                w_slots.append(4 * ((zl - way(core) * from_x) % 4) + 2 * (zh ^ s) + core)
    same = jnp.stack(w_slots)[:, None] == jnp.stack(g_slots)[None, :]
    which = jnp.sum(jnp.where(same, jnp.arange(16)[None, :], 0), axis=1).astype(jnp.int32)

    def ends(rank_both):
        rank_projected = rank_both[:, :rank_width]
        scaled_gradient = adapter_scale * rank_both[:, rank_width:]
        adapter_part = jnp.dot(scaled_gradient, down_adapter.astype(jnp.float32), precision=highest)
        inverse_order = 1.0 / lengths[0].astype(jnp.float32)
        down_gradient = (
            jnp.dot(scaled_gradient.T, projection_input.astype(jnp.float32), precision=highest)
            * inverse_order
        )[None]
        up_gradient = (
            adapter_scale
            * jnp.dot(rank_projected.T, masked_rows.astype(jnp.float32), precision=highest)
            * inverse_order
        )[None]
        return adapter_part, down_gradient, up_gradient

    before, beside = [], []
    for number, group in enumerate(ORDER, 1):
        names = []
        for entry in group:
            name, _, waits = entry.partition(":")
            takes, act = steps[name]
            given = [value[n] for n in takes]
            if name[0] != "+":
                given[0] = after(given[0], *before, *[value[n] for n in waits.split(",") if n])
                names.append(name)
            value[name] = act(*given)
        before, beside = [value[n] for n in names] + beside, []
        if number == 3:
            (total,) = partial_sum(number, which, value, g_places, w_places, None)
            beside = [total]
        if number == 4:
            total, g_aside, w_aside = partial_sum(number, which, value, g_places, w_places, total)
    adapter_part, down_gradient, up_gradient = ends(value["Ry4"])
    kept_column = kept.astype(jnp.float32)[:, None]
    grad_input = last_sum(which, value["F2"], value["SF"], g_aside, w_aside, total, kept_column, adapter_part)
    return (grad_input, down_gradient, up_gradient)


def solution(mesh):
    parts = Mesh(mesh.devices.reshape(SIZES), AXES)
    tenant, tensor = ("x", "zh", "c"), ("zl", "y")
    placed = (
        P(tenant, tensor),
        P(tenant, tensor),
        P(tenant, tensor),
        P(tenant, None, tensor),
        P(tenant, None, tensor),
        P(tenant),
    )
    return jax.shard_map(
        shards,
        mesh=parts,
        in_specs=placed,
        out_specs=(P(tenant, tensor), P(tenant, None, tensor), P(tenant, None, tensor)),
        check_vma=False,
    )
```
